32 devices in a mesh: occ: 32 (over z, y, x, core).
Axes of the slice: x: 2, y: 2, z: 4, core: 2. Of those that a mesh axis runs over, the one named last changes fastest.
Arguments:
- ri_factors: bfloat16 [32, 512, 1536], P('occ'), may hold values from -1.09375 to 1.09375
- occ_energy: float32 [32], P('occ'), may hold values from -1.5 to -0.3
- vir_energy: float32 [512], replicated, may hold values from 0.2 to 2.5
- partner: int32 [2, 32], P(None, 'occ'), may hold values from 0 to 31, as said below
- pair_weight: int32 [2, 32], P(None, 'occ'), may hold values from 1 to 2, as said below
Outputs:
- response: float32 [32, 512, 1536], P('occ')
- aux_density: float32 [1536, 1536], P('occ')
The draws below stay inside these ranges and needn't reach their ends.
Inputs may be any that keep to these rules, and one draw needn't show every extreme that they name: In each round the partner of orbital i is i XOR m for one nonzero m of that round, so partners pair up and the pair list is symmetric; in the first round m = 16. `pair_weight`: the two orbitals of a pair carry the same weight in a round.
All inputs are finite; a program needn't handle non-finite values.
Results may differ from the reference program's by a relative error of at most 0.0036.
Values may be sent and summed in bfloat16 or wider, within the bound.
A program may use at most 64 MiB of HBM per device.

```python
import jax
import jax.numpy as jnp
from jax import lax

V = 512
NAUX = 1536
ROUNDS = 2
NOCC = 32


def round_masks(key):
    later = jax.random.randint(jax.random.fold_in(key, 11), (ROUNDS - 1,), 1, NOCC).astype(jnp.int32)
    first = jnp.full((1,), NOCC // 2, jnp.int32)
    return jnp.concatenate([first, later]).astype(jnp.int32)


def draw_partner(key, part):
    masks = round_masks(key)
    orbitals = jnp.arange(NOCC, dtype=jnp.int32)
    return jnp.bitwise_xor(orbitals[None, :], masks[:, None]).astype(jnp.int32)


def draw_pair_weight(key, part):
    masks = round_masks(key)
    orbitals = jnp.arange(NOCC, dtype=jnp.int32)
    partners = jnp.bitwise_xor(orbitals[None, :], masks[:, None]).astype(jnp.int32)
    lowest = jnp.minimum(orbitals[None, :], partners)
    coins = jax.random.randint(jax.random.fold_in(key, 23), (ROUNDS, NOCC), 0, 2)
    weights = 1 + jnp.take_along_axis(coins, lowest, axis=1)
    rounds_col = jnp.arange(ROUNDS, dtype=jnp.int32)[:, None]
    weights = jnp.where((rounds_col == 0) & (lowest == 0), 2, weights)
    weights = jnp.where((rounds_col == 1) & (lowest == 0), 1, weights)
    return weights.astype(jnp.int32)


def block_scale(key, extent, cuts, least, top_value):
    loudness, own = 1.0, jax.random.fold_in(key, 6)
    for position, shards_of in cuts:
        draws = jnp.exp(jax.random.uniform(jax.random.fold_in(own, position), (shards_of,), jnp.float32, least / len(cuts), top_value / len(cuts)))
        loudness = loudness * jnp.repeat(draws, extent[position] // shards_of).reshape([-1 if axis == position else 1 for axis in range(len(extent))])
    return loudness


def centred(key, dims, deviation, most, pieces=(), kind=jnp.bfloat16):
    array = jax.random.normal(key, dims, jnp.float32) * deviation
    if len(pieces) > 0:
        array = block_scale(key, dims, pieces, -0.22, 0.18) * array
    return jnp.clip(array, min=-most, max=most).astype(kind)


def setup_inputs(seed: int = 0) -> dict:
    arg_keys = jax.random.split(jax.random.key(seed), 6)
    return {
        "ri_factors": centred(arg_keys[0], (NOCC, V, NAUX), 0.18, 1.09375, ((0, 32),)),
        "occ_energy": jnp.clip(-1.5 + 1.2 * jax.random.uniform(arg_keys[1], (NOCC,), jnp.float32) ** block_scale(arg_keys[1], (NOCC,), ((0, 32),), -0.2, 0.2), -1.5, -0.3),
        "vir_energy": jnp.clip(jax.random.uniform(arg_keys[2], (V,), jnp.float32, 0.2, 2.5), 0.2, 2.5),
        "partner": draw_partner(jax.random.fold_in(arg_keys[5], 71), 0),
        "pair_weight": draw_pair_weight(jax.random.fold_in(arg_keys[5], 71), 0),
    }


def reference(ri_factors, occ_energy, vir_energy, partner, pair_weight):
    def orbital(density, orbital_idx):
        own_block = ri_factors[orbital_idx]
        accumulated = jnp.zeros((V, NAUX), jnp.float32)
        for round_num in range(ROUNDS):
            other = partner[round_num, orbital_idx].astype(jnp.int32)
            fetched = lax.dynamic_index_in_dim(ri_factors, other, 0, keepdims=False)
            coulomb = jnp.dot(own_block, fetched.T, preferred_element_type=jnp.float32)
            denominator = occ_energy[orbital_idx] + occ_energy[other] - vir_energy[:, None] - vir_energy[None, :]
            amplitudes = coulomb / denominator
            combined = (2.0 * amplitudes - amplitudes.T).astype(jnp.bfloat16)
            weight_now = pair_weight[round_num, orbital_idx].astype(jnp.float32)
            response_part = (weight_now * jnp.dot(combined, fetched, preferred_element_type=jnp.float32)).astype(jnp.bfloat16)
            accumulated = accumulated + response_part.astype(jnp.float32)
            density = density + jnp.dot(response_part.T, own_block, preferred_element_type=jnp.float32)
        return density, accumulated

    density, responses = lax.scan(orbital, jnp.zeros((NAUX, NAUX), jnp.float32), jnp.arange(NOCC, dtype=jnp.int32))
    return responses, density / NOCC
```

```python
import functools

import jax
import jax.numpy as jnp
from jax import lax
from jax.experimental import pallas as pl
from jax.experimental.pallas import tpu as pltpu
from jax.sharding import PartitionSpec as P

ROUNDS = 2
AXIS = "occ"
CHAINS = 3
PIECES = 8


def chain_orders(bits):
    middle = list(range(1, bits - 1))
    orders = []
    for chain in range(CHAINS):
        turn = chain % max(len(middle), 1)
        orders.append([0] + middle[turn:] + middle[:turn] + ([bits - 1] if bits > 1 else []))
    return orders


def block_index(me, k, done, free):
    index = 0
    for bit in done:
        index = index + ((me // 2**bit) % 2) * 2**bit
    for place, bit in enumerate(free):
        index = index + ((k // 2**place) % 2) * 2**bit
    return index


def scatter_kernel(bits, orders, width, *refs):
    part_ref, out_ref, acc = refs[0], refs[1], refs[2]
    sends = refs[3 : 3 + bits]
    recvs = refs[3 + bits : 3 + 2 * bits]
    send_sem, recv_sem = refs[3 + 2 * bits], refs[4 + 2 * bits]
    me = lax.axis_index(AXIS)

    def peer(bit):
        own = (me // 2**bit) % 2
        return me + (1 - 2 * own) * 2**bit

    barrier = pltpu.get_barrier_semaphore()
    for bit in range(bits):
        pl.semaphore_signal(
            barrier, inc=1, device_id=(peer(bit),), device_id_type=pl.DeviceIdType.MESH
        )
    pl.semaphore_wait(barrier, bits)

    def copy(stage, chain):
        return pltpu.make_async_remote_copy(
            src_ref=sends[stage].at[chain],
            dst_ref=recvs[stage].at[chain],
            send_sem=send_sem.at[stage, chain],
            recv_sem=recv_sem.at[stage, chain],
            device_id=(peer(orders[chain][stage]),),
            device_id_type=pl.DeviceIdType.MESH,
        )

    def advance(stage, chain):
        order = orders[chain]
        bit = order[stage]
        before, free = order[:stage], order[stage + 1 :]
        columns = pl.ds(chain * width, width)
        count = 2 ** (bits - stage - 1)

        def arrived(side, k):
            return recvs[stage - 1][chain, side + 2 * k].astype(jnp.float32)

        def base(k, side):
            index = block_index(me, k, before, free) + side * 2**bit
            if stage == 0:
                return index, part_ref[index, :, columns]
            value = acc[index, :, columns] if stage > 1 else part_ref[index, :, columns]
            return index, value + arrived(side, k)

        mine = (me // 2**bit) % 2

        def send_one(k, _):
            index, value = base(k, 1 - mine)
            sends[stage][chain, k] = value.astype(jnp.bfloat16)
            return 0

        lax.fori_loop(0, count, send_one, 0)
        copy(stage, chain).start()
        if stage == 0:
            return

        def keep_one(k, _):
            index, value = base(k, mine)
            acc[index, :, columns] = value
            return 0

        lax.fori_loop(0, count, keep_one, 0)

    for chain in range(CHAINS):
        advance(0, chain)
    for stage in range(1, bits):
        for chain in range(CHAINS):
            copy(stage - 1, chain).wait()
            advance(stage, chain)
    for chain in range(CHAINS):
        columns = pl.ds(chain * width, width)
        copy(bits - 1, chain).wait()
        last = acc[me, :, columns] if bits > 1 else part_ref[me, :, columns]
        out_ref[:, columns] = last + recvs[bits - 1][chain, 0].astype(jnp.float32)


def density_scatter(partial):
    devices, rows, wide = partial.shape
    bits = devices.bit_length() - 1
    width = wide // CHAINS
    orders = chain_orders(bits)
    slots = [
        pltpu.VMEM((CHAINS, 2 ** (bits - stage - 1), rows, width), jnp.bfloat16)
        for stage in range(bits)
    ]
    return pl.pallas_call(
        functools.partial(scatter_kernel, bits, orders, width),
        out_shape=jax.ShapeDtypeStruct((rows, wide), jnp.float32),
        in_specs=[pl.BlockSpec(memory_space=pltpu.VMEM)],
        out_specs=pl.BlockSpec(memory_space=pltpu.VMEM),
        scratch_shapes=[pltpu.VMEM((devices, rows, wide), jnp.float32)]
        + slots
        + slots
        + [pltpu.SemaphoreType.DMA((bits, CHAINS)), pltpu.SemaphoreType.DMA((bits, CHAINS))],
        compiler_params=pltpu.CompilerParams(
            collective_id=0, has_side_effects=True, vmem_limit_bytes=58 * 2**20
        ),
    )(partial)


def exchange_kernel(bits, pieces, *refs):
    flags, own, energy, out0, out1, energies = refs[:6]
    stages = bits - 1
    held, arrived, held_e, arrived_e = refs[6:10]
    top_send, top_recv, low_send, low_recv = refs[10:14]
    me = lax.axis_index(AXIS)
    order = list(range(stages - 1, -1, -1))

    def peer(bit):
        mine = (me // 2**bit) % 2
        return me + (1 - 2 * mine) * 2**bit

    barrier = pltpu.get_barrier_semaphore()
    for bit in range(bits):
        pl.semaphore_signal(
            barrier, inc=1, device_id=(peer(bit),), device_id_type=pl.DeviceIdType.MESH
        )
    pl.semaphore_wait(barrier, bits)

    def remote(src, dst, send_sem, recv_sem, bit):
        return pltpu.make_async_remote_copy(
            src_ref=src,
            dst_ref=dst,
            send_sem=send_sem,
            recv_sem=recv_sem,
            device_id=(peer(bit),),
            device_id_type=pl.DeviceIdType.MESH,
        )

    def top(n):
        if n == pieces:
            src, dst = energy, energies.at[0]
        else:
            src, dst = own.at[n], out0.at[n]
        return remote(src, dst, top_send.at[n], top_recv.at[n], bits - 1)

    def lower(stage, n):
        if n == pieces:
            src, dst = held_e.at[stage], arrived_e.at[stage]
        else:
            src, dst = held.at[stage, n], arrived.at[stage, n]
        return remote(src, dst, low_send.at[stage, n], low_recv.at[stage, n], order[stage])

    def place(stage, n, value):
        if n == pieces:
            if stage == stages:
                energies[1] = value
            else:
                held_e[stage] = value
        elif stage == stages:
            out1[n] = value
        else:
            held[stage, n] = value
        if stage < stages:
            lower(stage, n).start()

    def enter(n):
        top(n).wait()
        taking = flags[bits - 1] == 1
        if n == pieces:
            place(0, n, jnp.where(taking, energies[0], energy[...]))
        else:
            place(0, n, jnp.where(taking, out0[n], own[n]))

    def step(stage, n):
        lower(stage, n).wait()
        taking = flags[order[stage]] == 1
        if n == pieces:
            place(stage + 1, n, jnp.where(taking, arrived_e[stage], held_e[stage]))
        else:
            place(stage + 1, n, jnp.where(taking, arrived[stage, n], held[stage, n]))

    sequence = [pieces] + list(range(pieces))
    ahead = 3
    for n in sequence[:ahead]:
        top(n).start()
    for tick in range(len(sequence) + stages):
        if tick < len(sequence):
            enter(sequence[tick])
            if tick + ahead < len(sequence):
                top(sequence[tick + ahead]).start()
        for stage in range(stages):
            place_in = tick - 1 - stage
            if 0 <= place_in < len(sequence):
                step(stage, sequence[place_in])


def exchange(flags, own, energy):
    bits = flags.shape[0]
    rows, wide = own.shape
    piece = rows // PIECES
    block = (PIECES, piece, wide)
    vmem = pl.BlockSpec(memory_space=pltpu.VMEM)
    tile = (8, 128)
    out0, out1, energies = pl.pallas_call(
        functools.partial(exchange_kernel, bits, PIECES),
        out_shape=[
            jax.ShapeDtypeStruct(block, own.dtype),
            jax.ShapeDtypeStruct(block, own.dtype),
            jax.ShapeDtypeStruct((ROUNDS,) + tile, jnp.float32),
        ],
        in_specs=[pl.BlockSpec(memory_space=pltpu.SMEM), vmem, vmem],
        out_specs=[vmem, vmem, vmem],
        scratch_shapes=[
            pltpu.VMEM((bits - 1,) + block, own.dtype),
            pltpu.VMEM((bits - 1,) + block, own.dtype),
            pltpu.VMEM((bits - 1,) + tile, jnp.float32),
            pltpu.VMEM((bits - 1,) + tile, jnp.float32),
            pltpu.SemaphoreType.DMA((PIECES + 1,)),
            pltpu.SemaphoreType.DMA((PIECES + 1,)),
            pltpu.SemaphoreType.DMA((bits - 1, PIECES + 1)),
            pltpu.SemaphoreType.DMA((bits - 1, PIECES + 1)),
        ],
        compiler_params=pltpu.CompilerParams(
            collective_id=1, has_side_effects=True, vmem_limit_bytes=48 * 2**20
        ),
    )(flags, own.reshape(block), jnp.broadcast_to(energy, tile))
    return (
        out0.reshape(rows, wide),
        out1.reshape(rows, wide),
        energies[0, 0, 0],
        energies[1, 0, 0],
    )


def body(ri_factors, occ_energy, vir_energy, partner, pair_weight):
    own = ri_factors[0]
    devices = lax.axis_size(AXIS)
    bits = devices.bit_length() - 1
    me = lax.axis_index(AXIS)
    rows = own.shape[1] // devices
    mask = jnp.bitwise_xor(partner[1, 0], me)
    flags = jnp.right_shift(mask, jnp.arange(bits, dtype=jnp.int32)) & 1

    fetched0, fetched1, energy0, energy1 = exchange(flags, own, occ_energy)
    fetched, energies = [fetched0, fetched1], [energy0, energy1]
    parts = []
    for turn in range(ROUNDS):
        coulomb = lax.dot_general(
            own, fetched[turn], (((1,), (1,)), ((), ())), preferred_element_type=jnp.float32
        )
        denominator = occ_energy[0] + energies[turn] - vir_energy[:, None] - vir_energy[None, :]
        amplitudes = coulomb / denominator
        combined = (2.0 * amplitudes - amplitudes.T).astype(jnp.bfloat16)
        weight = pair_weight[turn, 0].astype(jnp.float32)
        parts.append(
            (weight * jnp.dot(combined, fetched[turn], preferred_element_type=jnp.float32)).astype(
                jnp.bfloat16
            )
        )
    partial = sum(
        lax.dot_general(p, own, (((0,), (0,)), ((), ())), preferred_element_type=jnp.float32)
        for p in parts
    )
    density = density_scatter(partial.reshape(devices, rows, own.shape[1]))
    response = parts[0].astype(jnp.float32) + parts[1].astype(jnp.float32)
    return (response[None], density / float(devices))


def solution(mesh):
    placed = (P("occ", None, None), P("occ"), P(), P(None, "occ"), P(None, "occ"))
    return jax.shard_map(
        body,
        mesh=mesh,
        in_specs=placed,
        out_specs=(P("occ", None, None), P("occ", None)),
        check_vma=False,
    )
```

```python
import functools

import jax
import jax.numpy as jnp
from jax import lax
from jax.experimental import pallas as pl
from jax.experimental.pallas import tpu as pltpu
from jax.sharding import PartitionSpec as P

ROUNDS = 2
AXIS = "occ"
CHAINS = 3
PIECES = 16
GROUPS = 4
AHEAD = 6


def chain_orders(bits):
    middle = list(range(1, bits - 1))
    orders = []
    for chain in range(CHAINS):
        turn = chain % max(len(middle), 1)
        orders.append([0] + middle[turn:] + middle[:turn] + ([bits - 1] if bits > 1 else []))
    return orders


def block_index(me, k, done, free):
    index = 0
    for bit in done:
        index = index + ((me // 2**bit) % 2) * 2**bit
    for place, bit in enumerate(free):
        index = index + ((k // 2**place) % 2) * 2**bit
    return index


def scatter_kernel(bits, orders, width, *refs):
    inputs, refs = refs[: -4 - 2 * bits], refs[-4 - 2 * bits :]
    out_ref, acc = refs[0], refs[1]
    sends = refs[2 : 2 + bits]
    recvs = refs[2 + bits : 2 + 2 * bits]
    send_sem, recv_sem = refs[2 + 2 * bits], refs[3 + 2 * bits]
    fused = len(inputs) == 2
    part_ref = acc if fused else inputs[0]
    me = lax.axis_index(AXIS)

    def density_columns(chain):
        turned_ref, own_ref = inputs
        _, rows, _ = acc.shape
        columns = pl.ds(chain * width, width)

        def tile(t, _):
            spot = pl.ds(pl.multiple_of(t * 8 * rows, 8 * rows), 8 * rows)
            value = jnp.dot(
                turned_ref[0, spot, :], own_ref[:, columns], preferred_element_type=jnp.float32
            )
            for turn in range(1, ROUNDS):
                value += jnp.dot(
                    turned_ref[turn, spot, :],
                    own_ref[:, columns],
                    preferred_element_type=jnp.float32,
                )
            acc[pl.ds(t * 8, 8), :, columns] = value.reshape(8, rows, width)
            return 0

        lax.fori_loop(0, acc.shape[0] // 8, tile, 0)

    def peer(bit):
        own = (me // 2**bit) % 2
        return me + (1 - 2 * own) * 2**bit

    barrier = pltpu.get_barrier_semaphore()
    for bit in range(bits):
        pl.semaphore_signal(
            barrier, inc=1, device_id=(peer(bit),), device_id_type=pl.DeviceIdType.MESH
        )
    pl.semaphore_wait(barrier, bits)

    def copy(stage, chain):
        return pltpu.make_async_remote_copy(
            src_ref=sends[stage].at[chain],
            dst_ref=recvs[stage].at[chain],
            send_sem=send_sem.at[stage, chain],
            recv_sem=recv_sem.at[stage, chain],
            device_id=(peer(orders[chain][stage]),),
            device_id_type=pl.DeviceIdType.MESH,
        )

    def advance(stage, chain):
        order = orders[chain]
        bit = order[stage]
        before, free = order[:stage], order[stage + 1 :]
        columns = pl.ds(chain * width, width)
        count = 2 ** (bits - stage - 1)

        def arrived(side, k):
            return recvs[stage - 1][chain, side + 2 * k].astype(jnp.float32)

        def base(k, side):
            index = block_index(me, k, before, free) + side * 2**bit
            if stage == 0:
                return index, part_ref[index, :, columns]
            value = acc[index, :, columns] if stage > 1 else part_ref[index, :, columns]
            return index, value + arrived(side, k)

        mine = (me // 2**bit) % 2

        def send_one(k, _):
            index, value = base(k, 1 - mine)
            sends[stage][chain, k] = value.astype(jnp.bfloat16)
            return 0

        lax.fori_loop(0, count, send_one, 0)
        copy(stage, chain).start()
        if stage == 0:
            return

        def keep_one(k, _):
            index, value = base(k, mine)
            acc[index, :, columns] = value
            return 0

        lax.fori_loop(0, count, keep_one, 0)

    for chain in range(CHAINS):
        if fused:
            density_columns(chain)
        advance(0, chain)
    for stage in range(1, bits):
        for chain in range(CHAINS):
            copy(stage - 1, chain).wait()
            advance(stage, chain)
    for chain in range(CHAINS):
        columns = pl.ds(chain * width, width)
        copy(bits - 1, chain).wait()
        last = acc[me, :, columns] if bits > 1 else part_ref[me, :, columns]
        out_ref[:, columns] = last + recvs[bits - 1][chain, 0].astype(jnp.float32)


def density_scatter(turned, own):
    devices, wide = lax.axis_size(AXIS), own.shape[1]
    rows = wide // devices
    if rows % 16 == 0 and devices % 8 == 0:
        inputs = (turned, own)
    else:
        partial = sum(
            jnp.dot(turned[turn], own, preferred_element_type=jnp.float32)
            for turn in range(ROUNDS)
        )
        inputs = (partial.reshape(devices, rows, wide),)
    bits = devices.bit_length() - 1
    width = wide // CHAINS
    orders = chain_orders(bits)
    slots = [
        pltpu.VMEM((CHAINS, 2 ** (bits - stage - 1), rows, width), jnp.bfloat16)
        for stage in range(bits)
    ]
    return pl.pallas_call(
        functools.partial(scatter_kernel, bits, orders, width),
        out_shape=jax.ShapeDtypeStruct((rows, wide), jnp.float32),
        in_specs=[pl.BlockSpec(memory_space=pltpu.VMEM)] * len(inputs),
        out_specs=pl.BlockSpec(memory_space=pltpu.VMEM),
        scratch_shapes=[pltpu.VMEM((devices, rows, wide), jnp.float32)]
        + slots
        + slots
        + [pltpu.SemaphoreType.DMA((bits, CHAINS)), pltpu.SemaphoreType.DMA((bits, CHAINS))],
        compiler_params=pltpu.CompilerParams(
            collective_id=0, has_side_effects=True, vmem_limit_bytes=58 * 2**20
        ),
    )(*inputs)


def exchange_kernel(bits, *refs):
    flags, weights, own, energy, vir_row, vir_col, parts, turned = refs[:8]
    out0, out1, energies, coulomb, held, arrived, held_e, arrived_e = refs[8:16]
    top_send, top_recv, low_send, low_recv = refs[16:20]
    stages = bits - 1
    rows, wide = own.shape
    piece = rows // PIECES
    group = PIECES // GROUPS
    me = lax.axis_index(AXIS)
    order = list(range(stages - 1, -1, -1))
    blocks = [out0, out1]

    def span(n, count=1):
        return pl.ds(n * piece, count * piece)

    def peer(bit):
        mine = (me // 2**bit) % 2
        return me + (1 - 2 * mine) * 2**bit

    barrier = pltpu.get_barrier_semaphore()
    for bit in range(bits):
        pl.semaphore_signal(
            barrier, inc=1, device_id=(peer(bit),), device_id_type=pl.DeviceIdType.MESH
        )
    pl.semaphore_wait(barrier, bits)

    def remote(src, dst, send_sem, recv_sem, bit):
        return pltpu.make_async_remote_copy(
            src_ref=src,
            dst_ref=dst,
            send_sem=send_sem,
            recv_sem=recv_sem,
            device_id=(peer(bit),),
            device_id_type=pl.DeviceIdType.MESH,
        )

    def top(n):
        if n == PIECES:
            src, dst = energy, energies.at[0]
        else:
            src, dst = own.at[span(n)], out0.at[span(n)]
        return remote(src, dst, top_send.at[n], top_recv.at[n], bits - 1)

    def lower(stage, n):
        if n == PIECES:
            src, dst = held_e.at[stage], arrived_e.at[stage]
        else:
            src, dst = held.at[stage, span(n)], arrived.at[stage, span(n)]
        return remote(src, dst, low_send.at[stage, n], low_recv.at[stage, n], order[stage])

    def place(stage, n, value):
        if n == PIECES:
            if stage == stages:
                energies[1] = value
            else:
                held_e[stage] = value
        elif stage == stages:
            out1[span(n)] = value
        else:
            held[stage, span(n)] = value
        if stage < stages:
            lower(stage, n).start()

    def enter(n):
        top(n).wait()
        taking = flags[bits - 1] == 1
        if n == PIECES:
            place(0, n, jnp.where(taking, energies[0], energy[...]))
        else:
            place(0, n, jnp.where(taking, out0[span(n)], own[span(n)]))

    def step(stage, n):
        lower(stage, n).wait()
        taking = flags[order[stage]] == 1
        if n == PIECES:
            place(stage + 1, n, jnp.where(taking, arrived_e[stage], held_e[stage]))
        else:
            place(
                stage + 1, n, jnp.where(taking, arrived[stage, span(n)], held[stage, span(n)])
            )

    def coulomb_rows(turn, n):
        if n == PIECES or (n + 1) % group:
            return
        spot = span(n + 1 - group, group)
        coulomb[turn, spot, :] = lax.dot_general(
            blocks[turn][spot, :],
            own[...],
            (((1,), (1,)), ((), ())),
            preferred_element_type=jnp.float32,
        )

    def finish(turn):
        both = energy[0:1, 0:1] + energies[turn, 0:1, 0:1]
        flipped = coulomb[turn] / (both - vir_row[...] - vir_col[...])
        combined = (2.0 * flipped.T - flipped).astype(jnp.bfloat16)
        weight = weights[turn]
        width = wide // CHAINS

        def tile(t, _):
            spot = pl.ds(pl.multiple_of(t * width, width), width)
            product = jnp.dot(
                combined, blocks[turn][:, spot], preferred_element_type=jnp.float32
            )
            part = (weight * product).astype(jnp.bfloat16)
            parts[turn, :, spot] = part
            turned[turn, spot, :] = part.T
            return 0

        lax.fori_loop(0, CHAINS, tile, 0)

    sequence = [PIECES] + list(range(PIECES))
    for n in sequence[:AHEAD]:
        top(n).start()
    for tick in range(len(sequence) + stages):
        if tick < len(sequence):
            enter(sequence[tick])
            if tick + AHEAD < len(sequence):
                top(sequence[tick + AHEAD]).start()
        for stage in range(stages):
            place_in = tick - 1 - stage
            if 0 <= place_in < len(sequence):
                step(stage, sequence[place_in])
        if tick < len(sequence):
            coulomb_rows(0, sequence[tick])
        if tick == len(sequence):
            finish(0)
        if tick >= stages:
            coulomb_rows(1, sequence[tick - stages])
    finish(1)


def exchange(flags, weights, own, energy, vir_energy):
    bits = flags.shape[0]
    rows, wide = own.shape
    smem = pl.BlockSpec(memory_space=pltpu.SMEM)
    vmem = pl.BlockSpec(memory_space=pltpu.VMEM)
    tile = (8, 128)
    return pl.pallas_call(
        functools.partial(exchange_kernel, bits),
        out_shape=[
            jax.ShapeDtypeStruct((ROUNDS, rows, wide), own.dtype),
            jax.ShapeDtypeStruct((ROUNDS, wide, rows), own.dtype),
        ],
        in_specs=[smem, smem, vmem, vmem, vmem, vmem],
        out_specs=[vmem, vmem],
        scratch_shapes=[
            pltpu.VMEM((rows, wide), own.dtype),
            pltpu.VMEM((rows, wide), own.dtype),
            pltpu.VMEM((ROUNDS,) + tile, jnp.float32),
            pltpu.VMEM((ROUNDS, rows, rows), jnp.float32),
            pltpu.VMEM((bits - 1, rows, wide), own.dtype),
            pltpu.VMEM((bits - 1, rows, wide), own.dtype),
            pltpu.VMEM((bits - 1,) + tile, jnp.float32),
            pltpu.VMEM((bits - 1,) + tile, jnp.float32),
            pltpu.SemaphoreType.DMA((PIECES + 1,)),
            pltpu.SemaphoreType.DMA((PIECES + 1,)),
            pltpu.SemaphoreType.DMA((bits - 1, PIECES + 1)),
            pltpu.SemaphoreType.DMA((bits - 1, PIECES + 1)),
        ],
        compiler_params=pltpu.CompilerParams(
            collective_id=1, has_side_effects=True, vmem_limit_bytes=56 * 2**20
        ),
    )(
        flags,
        weights,
        own,
        jnp.broadcast_to(energy, tile),
        vir_energy.reshape(1, rows),
        vir_energy.reshape(rows, 1),
    )


def body(ri_factors, occ_energy, vir_energy, partner, pair_weight):
    own = ri_factors[0]
    devices = lax.axis_size(AXIS)
    bits = devices.bit_length() - 1
    me = lax.axis_index(AXIS)
    mask = jnp.bitwise_xor(partner[1, 0], me)
    flags = jnp.right_shift(mask, jnp.arange(bits, dtype=jnp.int32)) & 1
    weights = pair_weight[:, 0].astype(jnp.float32)
    parts, turned = exchange(flags, weights, own, occ_energy, vir_energy)
    density = density_scatter(turned, own)
    response = parts[0].astype(jnp.float32) + parts[1].astype(jnp.float32)
    return (response[None], density / float(devices))


def solution(mesh):
    placed = (P("occ", None, None), P("occ"), P(), P(None, "occ"), P(None, "occ"))
    return jax.shard_map(
        body,
        mesh=mesh,
        in_specs=placed,
        out_specs=(P("occ", None, None), P("occ", None)),
        check_vma=False,
    )
```

```python
import functools

import jax
import jax.numpy as jnp
from jax import lax
from jax.experimental import pallas as pl
from jax.experimental.pallas import tpu as pltpu
from jax.sharding import PartitionSpec as P

ROUNDS = 2
AXIS = "occ"
CHAINS = 3
PIECES = 16
GROUPS = 4
AHEAD = 6
LEAD = 3


def chain_orders(bits):
    middle = list(range(1, bits - 1))
    orders = []
    for chain in range(CHAINS):
        turn = chain % max(len(middle), 1)
        orders.append([0] + middle[turn:] + middle[:turn] + ([bits - 1] if bits > 1 else []))
    return orders


def block_index(me, k, done, free):
    index = 0
    for bit in done:
        index = index + ((me // 2**bit) % 2) * 2**bit
    for place, bit in enumerate(free):
        index = index + ((k // 2**place) % 2) * 2**bit
    return index


def scatter_kernel(bits, orders, width, *refs):
    inputs, refs = refs[: -4 - 2 * bits], refs[-4 - 2 * bits :]
    out_ref, acc = refs[0], refs[1]
    sends = refs[2 : 2 + bits]
    recvs = refs[2 + bits : 2 + 2 * bits]
    send_sem, recv_sem = refs[2 + 2 * bits], refs[3 + 2 * bits]
    fused = len(inputs) == 2
    part_ref = acc if fused else inputs[0]
    me = lax.axis_index(AXIS)

    def density_columns(chain):
        turned_ref, own_ref = inputs
        _, rows, _ = acc.shape
        columns = pl.ds(chain * width, width)

        def tile(t, _):
            spot = pl.ds(pl.multiple_of(t * 8 * rows, 8 * rows), 8 * rows)
            value = jnp.dot(
                turned_ref[0, spot, :], own_ref[:, columns], preferred_element_type=jnp.float32
            )
            for turn in range(1, ROUNDS):
                value += jnp.dot(
                    turned_ref[turn, spot, :],
                    own_ref[:, columns],
                    preferred_element_type=jnp.float32,
                )
            acc[pl.ds(t * 8, 8), :, columns] = value.reshape(8, rows, width)
            return 0

        lax.fori_loop(0, acc.shape[0] // 8, tile, 0)

    def peer(bit):
        own = (me // 2**bit) % 2
        return me + (1 - 2 * own) * 2**bit

    barrier = pltpu.get_barrier_semaphore()
    for bit in range(bits):
        pl.semaphore_signal(
            barrier, inc=1, device_id=(peer(bit),), device_id_type=pl.DeviceIdType.MESH
        )
    pl.semaphore_wait(barrier, bits)

    def copy(stage, chain):
        return pltpu.make_async_remote_copy(
            src_ref=sends[stage].at[chain],
            dst_ref=recvs[stage].at[chain],
            send_sem=send_sem.at[stage, chain],
            recv_sem=recv_sem.at[stage, chain],
            device_id=(peer(orders[chain][stage]),),
            device_id_type=pl.DeviceIdType.MESH,
        )

    def advance(stage, chain, keeping=False):
        order = orders[chain]
        bit = order[stage]
        before, free = order[:stage], order[stage + 1 :]
        columns = pl.ds(chain * width, width)
        count = 2 ** (bits - stage - 1)

        def arrived(side, k):
            return recvs[stage - 1][chain, side + 2 * k].astype(jnp.float32)

        def base(k, side):
            index = block_index(me, k, before, free) + side * 2**bit
            if stage == 0:
                return index, part_ref[index, :, columns]
            value = acc[index, :, columns] if stage > 1 else part_ref[index, :, columns]
            return index, value + arrived(side, k)

        mine = (me // 2**bit) % 2

        def send_one(k, _):
            index, value = base(k, 1 - mine)
            sends[stage][chain, k] = value.astype(jnp.bfloat16)
            return 0

        def keep_one(k, _):
            index, value = base(k, mine)
            acc[index, :, columns] = value
            return 0

        if keeping:
            lax.fori_loop(0, count, keep_one, 0)
        else:
            lax.fori_loop(0, count, send_one, 0)
            copy(stage, chain).start()

    for chain in range(CHAINS):
        if fused:
            density_columns(chain)
        advance(0, chain)
    for stage in range(1, bits):
        for chain in range(CHAINS):
            copy(stage - 1, chain).wait()
            advance(stage, chain)
        for chain in range(CHAINS):
            advance(stage, chain, keeping=True)
    for chain in range(CHAINS):
        columns = pl.ds(chain * width, width)
        copy(bits - 1, chain).wait()
        last = acc[me, :, columns] if bits > 1 else part_ref[me, :, columns]
        out_ref[:, columns] = last + recvs[bits - 1][chain, 0].astype(jnp.float32)


def density_scatter(turned, own):
    devices, wide = lax.axis_size(AXIS), own.shape[1]
    rows = wide // devices
    if rows % 16 == 0 and devices % 8 == 0:
        inputs = (turned, own)
    else:
        partial = sum(
            jnp.dot(turned[turn], own, preferred_element_type=jnp.float32)
            for turn in range(ROUNDS)
        )
        inputs = (partial.reshape(devices, rows, wide),)
    bits = devices.bit_length() - 1
    width = wide // CHAINS
    orders = chain_orders(bits)
    slots = [
        pltpu.VMEM((CHAINS, 2 ** (bits - stage - 1), rows, width), jnp.bfloat16)
        for stage in range(bits)
    ]
    return pl.pallas_call(
        functools.partial(scatter_kernel, bits, orders, width),
        out_shape=jax.ShapeDtypeStruct((rows, wide), jnp.float32),
        in_specs=[pl.BlockSpec(memory_space=pltpu.VMEM)] * len(inputs),
        out_specs=pl.BlockSpec(memory_space=pltpu.VMEM),
        scratch_shapes=[pltpu.VMEM((devices, rows, wide), jnp.float32)]
        + slots
        + slots
        + [pltpu.SemaphoreType.DMA((bits, CHAINS)), pltpu.SemaphoreType.DMA((bits, CHAINS))],
        compiler_params=pltpu.CompilerParams(
            collective_id=0, has_side_effects=True, vmem_limit_bytes=58 * 2**20
        ),
    )(*inputs)


def exchange_kernel(bits, across, hop, *refs):
    partner, weights, own, own_energy, vir_row, parts, turned = refs[:7]
    out0, out1, energy, energies, coulomb, vir_col = refs[7:13]
    held, arrived, held_e, arrived_e = refs[13:17]
    top_send, top_recv, low_send, low_recv = refs[17:21]
    rows, wide = own.shape
    piece = rows // PIECES
    group = PIECES // GROUPS
    me = lax.axis_index(AXIS)
    order = list(range(bits - 2 if hop else bits - 3, -1, -1))
    stages = len(order)
    blocks = [out0, out1]
    energy[...] = jnp.full(energy.shape, own_energy[0], jnp.float32)

    def span(n, count=1):
        return pl.ds(n * piece, count * piece)

    def peer(bit):
        mine = (me // 2**bit) % 2
        return me + (1 - 2 * mine) * 2**bit

    barrier = pltpu.get_barrier_semaphore()
    for bit in range(bits):
        pl.semaphore_signal(
            barrier, inc=1, device_id=(peer(bit),), device_id_type=pl.DeviceIdType.MESH
        )
    pl.semaphore_wait(barrier, bits)

    def remote(src, dst, send_sem, recv_sem, bit):
        return pltpu.make_async_remote_copy(
            src_ref=src,
            dst_ref=dst,
            send_sem=send_sem,
            recv_sem=recv_sem,
            device_id=(peer(bit),),
            device_id_type=pl.DeviceIdType.MESH,
        )

    def top(n):
        if n == PIECES:
            src, dst = energy, energies.at[0]
        else:
            src, dst = own.at[span(n)], out0.at[span(n)]
        return remote(src, dst, top_send.at[n], top_recv.at[n], bits - 1)

    def lower(stage, n):
        if n == PIECES:
            src, dst = held_e.at[stage], arrived_e.at[stage]
        else:
            src, dst = held.at[stage, span(n)], arrived.at[stage, span(n)]
        return remote(src, dst, low_send.at[stage, n], low_recv.at[stage, n], order[stage])

    def place(stage, n, value):
        if n == PIECES:
            if stage == stages:
                energies[1] = value
            else:
                held_e[stage] = value
        elif stage == stages:
            out1[span(n)] = value
        else:
            held[stage, span(n)] = value
        if stage < stages:
            lower(stage, n).start()

    def enter(n):
        if n == PIECES:
            place(0, n, energies[0] if across else energy[...])
        else:
            place(0, n, out0[span(n)] if across else own[span(n)])

    def step(stage, n):
        lower(stage, n).wait()
        bit = order[stage]
        if hop and bit == bits - 2:
            taking = True
        else:
            taking = (partner[1, 0] // 2**bit) % 2 != (me // 2**bit) % 2
        if n == PIECES:
            fresh, stale = arrived_e.at[stage], held_e.at[stage]
        else:
            fresh, stale = arrived.at[stage, span(n)], held.at[stage, span(n)]
        if taking is True:
            place(stage + 1, n, fresh[...])
        else:
            place(stage + 1, n, jnp.where(taking, fresh[...], stale[...]))

    def coulomb_rows(turn, n):
        if n == PIECES or (n + 1) % group:
            return
        spot = span(n + 1 - group, group)
        coulomb[turn, spot, :] = lax.dot_general(
            blocks[turn][spot, :],
            own[...],
            (((1,), (1,)), ((), ())),
            preferred_element_type=jnp.float32,
        )

    def finish(turn):
        both = energy[0:1, 0:1] + energies[turn, 0:1, 0:1]
        flipped = coulomb[turn] / (both - vir_row[...] - vir_col[:, 0:1])
        combined = (2.0 * flipped.T - flipped).astype(jnp.bfloat16)
        weight = weights[turn, 0].astype(jnp.float32)
        width = wide // CHAINS

        def tile(t, _):
            spot = pl.ds(pl.multiple_of(t * width, width), width)
            product = jnp.dot(
                combined, blocks[turn][:, spot], preferred_element_type=jnp.float32
            )
            part = (weight * product).astype(jnp.bfloat16)
            parts[turn, :, spot] = part
            turned[turn, spot, :] = part.T
            return 0

        lax.fori_loop(0, CHAINS, tile, 0)

    sequence = [PIECES] + list(range(PIECES))
    for n in sequence[:AHEAD]:
        top(n).start()
    count = len(sequence)
    vir_col[...] = jnp.broadcast_to(vir_row[...], (128, rows)).T

    def land(m):
        top(sequence[m]).wait()
        if m + AHEAD < count:
            top(sequence[m + AHEAD]).start()

    def hops(tick):
        for stage in range(stages):
            m = tick - 1 - stage
            if 0 <= m < count:
                step(stage, sequence[m])

    if across:
        for tick in range(count + stages):
            if tick < count:
                land(tick)
                enter(sequence[tick])
            hops(tick)
            if tick < count:
                coulomb_rows(0, sequence[tick])
            if tick == count:
                finish(0)
            if tick >= stages:
                coulomb_rows(1, sequence[tick - stages])
        finish(1)
    else:
        landed = 0
        for n in sequence[:LEAD]:
            enter(n)
        for tick in range(1, count + stages):
            if tick + LEAD - 1 < count:
                enter(sequence[tick + LEAD - 1])
            hops(tick)
            if tick >= stages:
                coulomb_rows(1, sequence[tick - stages])
            if tick % 2 and landed < count:
                land(landed)
                coulomb_rows(0, sequence[landed])
                landed += 1
        for m in range(landed, count):
            land(m)
            coulomb_rows(0, sequence[m])
            if m == landed + 1:
                finish(1)
        finish(0)


def exchange(across, hop, partner, weights, own, energy, vir_energy):
    bits = lax.axis_size(AXIS).bit_length() - 1
    rows, wide = own.shape
    smem = pl.BlockSpec(memory_space=pltpu.SMEM)
    vmem = pl.BlockSpec(memory_space=pltpu.VMEM)
    tile = (8, 128)
    return pl.pallas_call(
        functools.partial(exchange_kernel, bits, across, hop),
        out_shape=[
            jax.ShapeDtypeStruct((ROUNDS, rows, wide), own.dtype),
            jax.ShapeDtypeStruct((ROUNDS, wide, rows), own.dtype),
        ],
        in_specs=[smem, smem, vmem, smem, vmem],
        out_specs=[vmem, vmem],
        scratch_shapes=[
            pltpu.VMEM((rows, wide), own.dtype),
            pltpu.VMEM((rows, wide), own.dtype),
            pltpu.VMEM(tile, jnp.float32),
            pltpu.VMEM((ROUNDS,) + tile, jnp.float32),
            pltpu.VMEM((ROUNDS, rows, rows), jnp.float32),
            pltpu.VMEM((rows, 128), jnp.float32),
            pltpu.VMEM((bits - 1, rows, wide), own.dtype),
            pltpu.VMEM((bits - 1, rows, wide), own.dtype),
            pltpu.VMEM((bits - 1,) + tile, jnp.float32),
            pltpu.VMEM((bits - 1,) + tile, jnp.float32),
            pltpu.SemaphoreType.DMA((PIECES + 1,)),
            pltpu.SemaphoreType.DMA((PIECES + 1,)),
            pltpu.SemaphoreType.DMA((bits - 1, PIECES + 1)),
            pltpu.SemaphoreType.DMA((bits - 1, PIECES + 1)),
        ],
        compiler_params=pltpu.CompilerParams(
            collective_id=1 + 2 * across + hop, has_side_effects=True, vmem_limit_bytes=56 * 2**20
        ),
    )(
        partner,
        weights,
        own,
        energy,
        vir_energy.reshape(1, rows),
    )


def body(ri_factors, occ_energy, vir_energy, partner, pair_weight):
    own = ri_factors[0]
    devices = lax.axis_size(AXIS)
    bits = devices.bit_length() - 1
    me = lax.axis_index(AXIS)
    mask = jnp.bitwise_xor(partner[1, 0], me)
    forms = [
        functools.partial(exchange, across, hop) for across in (0, 1) for hop in (0, 1)
    ]
    parts, turned = lax.switch(
        jnp.right_shift(mask, bits - 2), forms, partner, pair_weight, own, occ_energy, vir_energy
    )
    density = density_scatter(turned, own)
    response = parts[0].astype(jnp.float32) + parts[1].astype(jnp.float32)
    return (response[None], density / float(devices))


def solution(mesh):
    placed = (P("occ", None, None), P("occ"), P(), P(None, "occ"), P(None, "occ"))
    return jax.shard_map(
        body,
        mesh=mesh,
        in_specs=placed,
        out_specs=(P("occ", None, None), P("occ", None)),
        check_vma=False,
    )
```

```python
import functools

import jax
import jax.numpy as jnp
from jax import lax
from jax.experimental import pallas as pl
from jax.experimental.pallas import tpu as pltpu
from jax.sharding import PartitionSpec as P

ROUNDS = 2
AXIS = "occ"
CHAINS = 3
PIECES = 16
GROUPS = 4
AHEAD = 6
LEAD = 3


def chain_orders(bits):
    middle = list(range(1, bits - 1))
    orders = []
    for chain in range(CHAINS):
        turn = chain % max(len(middle), 1)
        orders.append([0] + middle[turn:] + middle[:turn] + ([bits - 1] if bits > 1 else []))
    return orders


def block_index(me, k, done, free):
    index = 0
    for bit in done:
        index = index + ((me // 2**bit) % 2) * 2**bit
    for place, bit in enumerate(free):
        index = index + ((k // 2**place) % 2) * 2**bit
    return index


def scatter_kernel(bits, orders, width, *refs):
    inputs, refs = refs[: -4 - 2 * bits], refs[-4 - 2 * bits :]
    out_ref, acc = refs[0], refs[1]
    sends = refs[2 : 2 + bits]
    recvs = refs[2 + bits : 2 + 2 * bits]
    send_sem, recv_sem = refs[2 + 2 * bits], refs[3 + 2 * bits]
    fused = len(inputs) == 2
    part_ref = acc if fused else inputs[0]
    me = lax.axis_index(AXIS)

    def density_columns(chain):
        turned_ref, own_ref = inputs
        _, rows, _ = acc.shape
        columns = pl.ds(chain * width, width)

        def tile(t, _):
            spot = pl.ds(pl.multiple_of(t * 8 * rows, 8 * rows), 8 * rows)
            value = jnp.dot(
                turned_ref[0, spot, :], own_ref[:, columns], preferred_element_type=jnp.float32
            )
            for turn in range(1, ROUNDS):
                value += jnp.dot(
                    turned_ref[turn, spot, :],
                    own_ref[:, columns],
                    preferred_element_type=jnp.float32,
                )
            acc[pl.ds(t * 8, 8), :, columns] = value.reshape(8, rows, width)
            return 0

        lax.fori_loop(0, acc.shape[0] // 8, tile, 0)

    def peer(bit):
        own = (me // 2**bit) % 2
        return me + (1 - 2 * own) * 2**bit

    barrier = pltpu.get_barrier_semaphore()
    for bit in range(bits):
        pl.semaphore_signal(
            barrier, inc=1, device_id=(peer(bit),), device_id_type=pl.DeviceIdType.MESH
        )
    pl.semaphore_wait(barrier, bits)

    def copy(stage, chain):
        return pltpu.make_async_remote_copy(
            src_ref=sends[stage].at[chain],
            dst_ref=recvs[stage].at[chain],
            send_sem=send_sem.at[stage, chain],
            recv_sem=recv_sem.at[stage, chain],
            device_id=(peer(orders[chain][stage]),),
            device_id_type=pl.DeviceIdType.MESH,
        )

    def advance(stage, chain, keeping=False):
        order = orders[chain]
        bit = order[stage]
        before, free = order[:stage], order[stage + 1 :]
        columns = pl.ds(chain * width, width)
        count = 2 ** (bits - stage - 1)

        def arrived(side, k):
            return recvs[stage - 1][chain, side + 2 * k].astype(jnp.float32)

        def base(k, side):
            index = block_index(me, k, before, free) + side * 2**bit
            if stage == 0:
                return index, part_ref[index, :, columns]
            value = acc[index, :, columns] if stage > 1 else part_ref[index, :, columns]
            return index, value + arrived(side, k)

        mine = (me // 2**bit) % 2

        def send_one(k, _):
            index, value = base(k, 1 - mine)
            sends[stage][chain, k] = value.astype(jnp.bfloat16)
            return 0

        def keep_one(k, _):
            index, value = base(k, mine)
            acc[index, :, columns] = value
            return 0

        if keeping:
            lax.fori_loop(0, count, keep_one, 0)
        else:
            lax.fori_loop(0, count, send_one, 0)
            copy(stage, chain).start()

    for chain in range(CHAINS):
        if fused:
            density_columns(chain)
        advance(0, chain)
    for stage in range(1, bits):
        for chain in range(CHAINS):
            copy(stage - 1, chain).wait()
            advance(stage, chain)
        for chain in range(CHAINS):
            advance(stage, chain, keeping=True)
    for chain in range(CHAINS):
        columns = pl.ds(chain * width, width)
        copy(bits - 1, chain).wait()
        last = acc[me, :, columns] if bits > 1 else part_ref[me, :, columns]
        out_ref[:, columns] = last + recvs[bits - 1][chain, 0].astype(jnp.float32)


def density_scatter(turned, own):
    devices, wide = lax.axis_size(AXIS), own.shape[1]
    rows = wide // devices
    if rows % 16 == 0 and devices % 8 == 0:
        inputs = (turned, own)
    else:
        partial = sum(
            jnp.dot(turned[turn], own, preferred_element_type=jnp.float32)
            for turn in range(ROUNDS)
        )
        inputs = (partial.reshape(devices, rows, wide),)
    bits = devices.bit_length() - 1
    width = wide // CHAINS
    orders = chain_orders(bits)
    slots = [
        pltpu.VMEM((CHAINS, 2 ** (bits - stage - 1), rows, width), jnp.bfloat16)
        for stage in range(bits)
    ]
    return pl.pallas_call(
        functools.partial(scatter_kernel, bits, orders, width),
        out_shape=jax.ShapeDtypeStruct((rows, wide), jnp.float32),
        in_specs=[pl.BlockSpec(memory_space=pltpu.VMEM)] * len(inputs),
        out_specs=pl.BlockSpec(memory_space=pltpu.VMEM),
        scratch_shapes=[pltpu.VMEM((devices, rows, wide), jnp.float32)]
        + slots
        + slots
        + [pltpu.SemaphoreType.DMA((bits, CHAINS)), pltpu.SemaphoreType.DMA((bits, CHAINS))],
        compiler_params=pltpu.CompilerParams(
            collective_id=0, has_side_effects=True, vmem_limit_bytes=58 * 2**20
        ),
    )(*inputs)


def exchange_kernel(bits, across, hop, *refs):
    partner, weights, own, own_energy, vir_row, parts, turned = refs[:7]
    out0, out1, energy, energies, coulomb, vir_col = refs[7:13]
    held, arrived, held_e, arrived_e = refs[13:17]
    top_send, top_recv, low_send, low_recv, combined = refs[17:22]
    rows, wide = own.shape
    piece = rows // PIECES
    group = PIECES // GROUPS
    me = lax.axis_index(AXIS)
    order = list(range(bits - 2 if hop else bits - 3, -1, -1))
    stages = len(order)
    blocks = [out0, out1]
    energy[...] = jnp.full(energy.shape, own_energy[0], jnp.float32)

    def span(n, count=1):
        return pl.ds(n * piece, count * piece)

    def peer(bit):
        mine = (me // 2**bit) % 2
        return me + (1 - 2 * mine) * 2**bit

    barrier = pltpu.get_barrier_semaphore()
    for bit in range(bits):
        pl.semaphore_signal(
            barrier, inc=1, device_id=(peer(bit),), device_id_type=pl.DeviceIdType.MESH
        )
    pl.semaphore_wait(barrier, bits)

    def remote(src, dst, send_sem, recv_sem, bit):
        return pltpu.make_async_remote_copy(
            src_ref=src,
            dst_ref=dst,
            send_sem=send_sem,
            recv_sem=recv_sem,
            device_id=(peer(bit),),
            device_id_type=pl.DeviceIdType.MESH,
        )

    def top(n):
        if n == PIECES:
            src, dst = energy, energies.at[0]
        else:
            src, dst = own.at[span(n)], out0.at[span(n)]
        return remote(src, dst, top_send.at[n], top_recv.at[n], bits - 1)

    def lower(stage, n):
        if n == PIECES:
            src, dst = held_e.at[stage], arrived_e.at[stage]
        else:
            src, dst = held.at[stage, span(n)], arrived.at[stage, span(n)]
        return remote(src, dst, low_send.at[stage, n], low_recv.at[stage, n], order[stage])

    def place(stage, n, value):
        if n == PIECES:
            if stage == stages:
                energies[1] = value
            else:
                held_e[stage] = value
        elif stage == stages:
            out1[span(n)] = value
        else:
            held[stage, span(n)] = value
        if stage < stages:
            lower(stage, n).start()

    def enter(n):
        if n == PIECES:
            place(0, n, energies[0] if across else energy[...])
        else:
            place(0, n, out0[span(n)] if across else own[span(n)])

    def step(stage, n):
        lower(stage, n).wait()
        bit = order[stage]
        if hop and bit == bits - 2:
            taking = True
        else:
            taking = (partner[1, 0] // 2**bit) % 2 != (me // 2**bit) % 2
        if n == PIECES:
            fresh, stale = arrived_e.at[stage], held_e.at[stage]
        else:
            fresh, stale = arrived.at[stage, span(n)], held.at[stage, span(n)]
        if taking is True:
            place(stage + 1, n, fresh[...])
        else:
            place(stage + 1, n, jnp.where(taking, fresh[...], stale[...]))

    def coulomb_rows(turn, n):
        if n == PIECES or (n + 1) % group:
            return
        spot = span(n + 1 - group, group)
        coulomb[turn, spot, :] = lax.dot_general(
            blocks[turn][spot, :],
            own[...],
            (((1,), (1,)), ((), ())),
            preferred_element_type=jnp.float32,
        )

    def combine(turn):
        both = energy[0:1, 0:1] + energies[turn, 0:1, 0:1]
        flipped = coulomb[turn] / (both - vir_row[...] - vir_col[:, 0:1])
        combined[...] = (2.0 * flipped.T - flipped).astype(jnp.bfloat16)

    def finish(turn):
        weight = weights[turn, 0].astype(jnp.float32)
        width = wide // CHAINS

        def tile(t, _):
            spot = pl.ds(pl.multiple_of(t * width, width), width)
            product = jnp.dot(
                combined[...], blocks[turn][:, spot], preferred_element_type=jnp.float32
            )
            part = (weight * product).astype(jnp.bfloat16)
            parts[turn, :, spot] = part
            turned[turn, spot, :] = part.T
            return 0

        lax.fori_loop(0, CHAINS, tile, 0)

    sequence = [PIECES] + list(range(PIECES))
    for n in sequence[:AHEAD]:
        top(n).start()
    count = len(sequence)
    vir_col[...] = jnp.broadcast_to(vir_row[...], (128, rows)).T

    def land(m):
        top(sequence[m]).wait()
        if m + AHEAD < count:
            top(sequence[m + AHEAD]).start()

    def hops(tick):
        for stage in range(stages):
            m = tick - 1 - stage
            if 0 <= m < count:
                step(stage, sequence[m])

    if across:
        for tick in range(count + stages):
            if tick < count:
                land(tick)
                enter(sequence[tick])
            hops(tick)
            if tick < count:
                coulomb_rows(0, sequence[tick])
            if tick == count:
                combine(0)
            if tick == count + 1:
                finish(0)
            if tick >= stages:
                coulomb_rows(1, sequence[tick - stages])
        combine(1)
        finish(1)
    else:
        landed = 0
        for n in sequence[:LEAD]:
            enter(n)
        for tick in range(1, count + stages):
            if tick + LEAD - 1 < count:
                enter(sequence[tick + LEAD - 1])
            hops(tick)
            if tick >= stages:
                coulomb_rows(1, sequence[tick - stages])
            if tick % 2 and landed < count:
                land(landed)
                coulomb_rows(0, sequence[landed])
                landed += 1
        for m in range(landed, count):
            land(m)
            coulomb_rows(0, sequence[m])
            if m == landed + 1:
                combine(1)
                finish(1)
        combine(0)
        finish(0)


def exchange(across, hop, partner, weights, own, energy, vir_energy):
    bits = lax.axis_size(AXIS).bit_length() - 1
    rows, wide = own.shape
    smem = pl.BlockSpec(memory_space=pltpu.SMEM)
    vmem = pl.BlockSpec(memory_space=pltpu.VMEM)
    tile = (8, 128)
    return pl.pallas_call(
        functools.partial(exchange_kernel, bits, across, hop),
        out_shape=[
            jax.ShapeDtypeStruct((ROUNDS, rows, wide), own.dtype),
            jax.ShapeDtypeStruct((ROUNDS, wide, rows), own.dtype),
        ],
        in_specs=[smem, smem, vmem, smem, vmem],
        out_specs=[vmem, vmem],
        scratch_shapes=[
            pltpu.VMEM((rows, wide), own.dtype),
            pltpu.VMEM((rows, wide), own.dtype),
            pltpu.VMEM(tile, jnp.float32),
            pltpu.VMEM((ROUNDS,) + tile, jnp.float32),
            pltpu.VMEM((ROUNDS, rows, rows), jnp.float32),
            pltpu.VMEM((rows, 128), jnp.float32),
            pltpu.VMEM((bits - 1, rows, wide), own.dtype),
            pltpu.VMEM((bits - 1, rows, wide), own.dtype),
            pltpu.VMEM((bits - 1,) + tile, jnp.float32),
            pltpu.VMEM((bits - 1,) + tile, jnp.float32),
            pltpu.SemaphoreType.DMA((PIECES + 1,)),
            pltpu.SemaphoreType.DMA((PIECES + 1,)),
            pltpu.SemaphoreType.DMA((bits - 1, PIECES + 1)),
            pltpu.SemaphoreType.DMA((bits - 1, PIECES + 1)),
            pltpu.VMEM((rows, rows), jnp.bfloat16),
        ],
        compiler_params=pltpu.CompilerParams(
            collective_id=1 + 2 * across + hop, has_side_effects=True, vmem_limit_bytes=56 * 2**20
        ),
    )(
        partner,
        weights,
        own,
        energy,
        vir_energy.reshape(1, rows),
    )


def body(ri_factors, occ_energy, vir_energy, partner, pair_weight):
    own = ri_factors[0]
    devices = lax.axis_size(AXIS)
    bits = devices.bit_length() - 1
    me = lax.axis_index(AXIS)
    mask = jnp.bitwise_xor(partner[1, 0], me)
    forms = [
        functools.partial(exchange, across, hop) for across in (0, 1) for hop in (0, 1)
    ]
    parts, turned = lax.switch(
        jnp.right_shift(mask, bits - 2), forms, partner, pair_weight, own, occ_energy, vir_energy
    )
    density = density_scatter(turned, own)
    response = parts[0].astype(jnp.float32) + parts[1].astype(jnp.float32)
    return (response[None], density / float(devices))


def solution(mesh):
    placed = (P("occ", None, None), P("occ"), P(), P(None, "occ"), P(None, "occ"))
    return jax.shard_map(
        body,
        mesh=mesh,
        in_specs=placed,
        out_specs=(P("occ", None, None), P("occ", None)),
        check_vma=False,
    )
```
